32 devices in a mesh: section: 2 (over x), batch: 16 (over z, y, core).
Axes of the slice: x: 2, y: 2, z: 4, core: 2. Of those that a mesh axis runs over, the one named last changes fastest.
Arguments:
- tokens: bfloat16 [2, 16, 1024, 384], P(None, 'batch'), may hold values from -6 to 6
- segments: int32 [2, 16, 1024], P(None, 'batch'), may hold values from 0 to 23, never falling along the last dimension, each value on 1 to 64 neighbouring positions
- cotangent: bfloat16 [2, 16, 1024, 384], P(None, 'batch'), may hold values from -6 to 6
- w_qkv: bfloat16 [2, 384, 1152], P('section'), may hold values from -0.3125 to 0.3125
- b_qkv: bfloat16 [2, 1152], P('section'), may hold values from -1.796875 to 1.796875
- w_out: bfloat16 [2, 384, 384], P('section'), may hold values from -0.875 to 0.875
- b_out: bfloat16 [2, 384], P('section'), may hold values from -3 to 3
- norm1_gain: bfloat16 [2, 384], P('section'), may hold values from 0.25 to 1.75
- norm1_bias: bfloat16 [2, 384], P('section'), may hold values from -1.796875 to 1.796875
- w_up: bfloat16 [2, 384, 1536], P('section'), may hold values from -0.3125 to 0.3125
- b_up: bfloat16 [2, 1536], P('section'), may hold values from -3 to 3
- w_down: bfloat16 [2, 1536, 384], P('section'), may hold values from -0.15625 to 0.15625
- b_down: bfloat16 [2, 384], P('section'), may hold values from -3 to 3
- norm2_gain: bfloat16 [2, 384], P('section'), may hold values from 0.25 to 1.75
- norm2_bias: bfloat16 [2, 384], P('section'), may hold values from -1.796875 to 1.796875
Outputs:
- layer_out: bfloat16 [2, 2, 16, 1024, 384], P('section', None, 'batch')
- layer_in_grad: bfloat16 [2, 2, 16, 1024, 384], P('section', None, 'batch')
- grad_w_qkv: float32 [2, 384, 1152], P('section')
- grad_b_qkv: float32 [2, 1152], P('section')
- grad_w_out: float32 [2, 384, 384], P('section')
- grad_b_out: float32 [2, 384], P('section')
- grad_norm1_gain: float32 [2, 384], P('section')
- grad_norm1_bias: float32 [2, 384], P('section')
- grad_w_up: float32 [2, 384, 1536], P('section')
- grad_b_up: float32 [2, 1536], P('section')
- grad_w_down: float32 [2, 1536, 384], P('section')
- grad_b_down: float32 [2, 384], P('section')
- grad_norm2_gain: float32 [2, 384], P('section')
- grad_norm2_bias: float32 [2, 384], P('section')
The draws below stay inside these ranges and needn't reach their ends.
Inputs may be any that keep to these rules, and one draw needn't show every extreme that they name: `segments`: along each row the ids never fall; a document covers 1 to 64 consecutive positions.
All inputs are finite; a program needn't handle non-finite values.
Results may differ from the reference program's by a relative error of at most 0.015.
Values may be sent and summed in bfloat16 or wider, within the bound.
A program may use at most 320 MiB of HBM per device.

```python
import math
import jax
import jax.numpy as jnp
import numpy as np
from jax import lax

D = 384
FF = 1536
HEADS = 6
HEAD_DIM = 64
SEQ = 1024
QBLOCK = 512
DOCS = 24
MICRO = 2
DOC_MOST = 64
ROWS = 16


def levels(own_key, extent, pieces, low, top_value):
    level, own = 1.0, jax.random.fold_in(own_key, 6)
    for dim, shards_of in pieces:
        heights = jnp.exp(jax.random.uniform(jax.random.fold_in(own, dim), (shards_of,), jnp.float32, low / len(pieces), top_value / len(pieces)))
        level = level * jnp.repeat(heights, extent[dim] // shards_of).reshape([-1 if axis == dim else 1 for axis in range(len(extent))])
    return level


def length_profile(number_of, total, bound, skew):
    weights = [(1 << 20) // math.isqrt(grade ** skew) + 1 for grade in range(2, number_of + 1)]
    spare, given = total - bound - (number_of - 1), [1] * (number_of - 1)
    while spare > 0:
        movable = [i for i in range(number_of - 1) if given[i] < bound]
        whole, left = sum([weights[i] for i in movable]), spare
        for i in movable:
            extra = min(bound - given[i], max(1, left * weights[i] // whole), spare)
            given[i] = given[i] + extra
            spare = spare - extra
    return np.array([bound] + given)


def uneven_parts(stream_key, count, total, limit, skew):
    if count == 2:
        one = jax.random.randint(stream_key, (), max(1, total - limit), min(limit, total - 1) + 1)
        return jnp.stack([one, total - one])
    lengths = jnp.asarray(length_profile(count, total, limit, skew), jnp.int32)
    pairs = (count - 1) // 2
    source_of, taker = lengths[1:1 + 2 * pairs:2], lengths[2:2 + 2 * pairs:2]
    slack = jnp.minimum(source_of - 1, limit - taker)
    shifted = jax.random.randint(jax.random.fold_in(stream_key, 1), (pairs,), 0, 1 << 20) % (slack + 1)
    lengths = lengths.at[1:1 + 2 * pairs:2].set(source_of - shifted).at[2:2 + 2 * pairs:2].set(taker + shifted)
    return lengths[jax.random.permutation(jax.random.fold_in(stream_key, 2), count)]


def gaussian(key, dims, scale, limit, shards=(), kind=jnp.bfloat16):
    level = levels(key, dims, shards, -0.22, 0.18) if shards else 1.0
    entries = jax.random.normal(key, dims, jnp.float32) * scale * level
    return jnp.minimum(jnp.maximum(entries, -limit), limit).astype(kind)


def setup_inputs(seed: int = 0) -> dict:
    key_of = jax.random.split(jax.random.key(seed), 16)
    return {
        "tokens": gaussian(key_of[0], (MICRO, ROWS, SEQ, D), 1.0, 6.0, ((1, 16),)),
        "segments": jax.vmap(lambda own: jnp.searchsorted(jnp.cumsum(uneven_parts(own, DOCS, SEQ, DOC_MOST, 2)), jnp.arange(SEQ), side="right"))(jax.random.split(key_of[1], MICRO * ROWS)).reshape((MICRO, ROWS, SEQ)).astype(jnp.int32),
        "cotangent": gaussian(key_of[2], (MICRO, ROWS, SEQ, D), 1.0, 6.0, ((1, 16),)),
        "w_qkv": gaussian(key_of[3], (2, D, 3 * D), D ** -0.5, 0.3125, ((0, 2),)),
        "b_qkv": gaussian(key_of[4], (2, 3 * D), 0.3, 1.796875, ((0, 2),)),
        "w_out": gaussian(key_of[5], (2, D, D), (D // 8) ** -0.5, 0.875, ((0, 2),)),
        "b_out": gaussian(key_of[6], (2, D), 0.5, 3.0, ((0, 2),)),
        "norm1_gain": jnp.clip(1.0 + 0.15 * jax.random.normal(key_of[7], (2, D), jnp.float32), 0.25, 1.75).astype(jnp.bfloat16),
        "norm1_bias": gaussian(key_of[8], (2, D), 0.3, 1.796875, ((0, 2),)),
        "w_up": gaussian(key_of[9], (2, D, FF), D ** -0.5, 0.3125, ((0, 2),)),
        "b_up": gaussian(key_of[10], (2, FF), 0.5, 3.0, ((0, 2),)),
        "w_down": gaussian(key_of[11], (2, FF, D), FF ** -0.5, 0.15625, ((0, 2),)),
        "b_down": gaussian(key_of[12], (2, D), 0.5, 3.0, ((0, 2),)),
        "norm2_gain": jnp.clip(1.0 + 0.15 * jax.random.normal(key_of[13], (2, D), jnp.float32), 0.25, 1.75).astype(jnp.bfloat16),
        "norm2_bias": gaussian(key_of[14], (2, D), 0.3, 1.796875, ((0, 2),)),
    }


@jax.custom_vjp
def low(v):
    return lax.optimization_barrier(v.astype(jnp.bfloat16)).astype(jnp.float32)

@jax.custom_vjp
def low_back(v):
    return v

def low_keep(v):
    return (low(v), None)

def low_pass(kept, grad):
    return (grad,)

def back_keep(v):
    return (v, None)

def back_low(kept, grad):
    return (low(grad),)
low.defvjp(low_keep, low_pass)
low_back.defvjp(back_keep, back_low)
HIGHEST = lax.Precision.HIGHEST
NEG_LARGE = -1e+30
NORM_EPS = 1e-12

def rotary_tables(segment):
    length = segment.shape[-1]
    index = jnp.arange(length, dtype=jnp.int32)
    change = jnp.concatenate([jnp.ones(segment.shape[:-1] + (1,), jnp.bool_), segment[..., 1:] != segment[..., :-1]], axis=-1)
    start = lax.cummax(jnp.where(change, index, 0).astype(jnp.int32), axis=segment.ndim - 1)
    offset = (index - start).astype(jnp.float32).reshape(-1, 1)
    channel = jnp.arange(HEADS * HEAD_DIM, dtype=jnp.int32)
    pair_rank = (channel % HEAD_DIM // 2).astype(jnp.float32)
    freq = jnp.power(jnp.float32(10000.0), -2.0 * pair_rank / HEAD_DIM)
    angle = offset * freq
    signed = jnp.where(channel % 2 == 0, -1.0, 1.0).astype(jnp.float32)
    return (jnp.cos(angle), jnp.sin(angle) * signed)

def partner(value):
    count = value.shape[0]
    return value.reshape(count, -1, 2)[:, :, ::-1].reshape(count, -1)

def turn(value, cosine, sine_signed):
    return value * cosine + partner(value) * sine_signed

def norm_rows(value, gain, bias):
    centre = lax.optimization_barrier(jnp.mean(value, axis=-1, keepdims=True))
    centred = value - centre
    spread = lax.optimization_barrier(jnp.mean(centred * centred, axis=-1, keepdims=True))
    return centred * lax.rsqrt(spread + NORM_EPS) * gain + bias

def attention(queries, keys_rot, values, segment):
    length = segment.shape[0]
    blocks = length // QBLOCK
    q_heads = queries.reshape(blocks, QBLOCK, HEADS, HEAD_DIM)
    k_heads = keys_rot.reshape(length, HEADS, HEAD_DIM)
    v_heads = values.reshape(length, HEADS, HEAD_DIM)
    seg_blocks = segment.reshape(blocks, QBLOCK)

    def one_block(item):
        q_block, seg_block = item
        scores = low_back(jnp.einsum('qhd,khd->hqk', q_block, k_heads, precision=HIGHEST) * HEAD_DIM ** (-0.5))
        same = seg_block[:, None] == segment[None, :]
        scores = jnp.where(same[None], scores, NEG_LARGE)
        attn_probs = jax.nn.softmax(scores, axis=-1)
        return jnp.einsum('hqk,khd->qhd', low(attn_probs), v_heads, precision=HIGHEST)
    mapped = lax.map(jax.checkpoint(one_block), (q_heads, seg_blocks))
    return mapped.reshape(length, HEADS * HEAD_DIM)

def layer(params, entering, segment):
    w_qkv, b_qkv, w_out, b_out, gain_one, bias_one, w_up, b_up, w_down, b_down, gain_two, bias_two = params
    entering = low_back(entering)
    cosine, sine_signed = rotary_tables(segment)
    projected = low_back(jnp.dot(entering, w_qkv, precision=HIGHEST) + b_qkv)
    queries = low(turn(projected[:, :D], cosine, sine_signed))
    keys_rot = low(turn(projected[:, D:2 * D], cosine, sine_signed))
    values = low(projected[:, 2 * D:])
    context = low(low_back(attention(queries, keys_rot, values, segment)))
    mixed = low_back(jnp.dot(context, w_out, precision=HIGHEST) + b_out)
    hidden = norm_rows(entering + mixed, gain_one, bias_one)
    upward = low_back(jnp.dot(low(hidden), w_up, precision=HIGHEST) + b_up)
    active = low(jax.nn.gelu(upward, approximate=False))
    downward = low_back(jnp.dot(active, w_down, precision=HIGHEST) + b_down)
    return norm_rows(hidden + downward, gain_two, bias_two)

def reference(tokens, segments, cotangent, w_qkv, b_qkv, w_out, b_out, norm1_gain, norm1_bias, w_up, b_up, w_down, b_down, norm2_gain, norm2_bias):
    weights = tuple((w.astype(jnp.float32) for w in (w_qkv, b_qkv, w_out, b_out, norm1_gain, norm1_bias, w_up, b_up, w_down, b_down, norm2_gain, norm2_bias)))
    lower_params = tuple((w[0] for w in weights))
    upper_params = tuple((w[1] for w in weights))
    flat_tokens = tokens.reshape(MICRO * ROWS, SEQ, D)
    flat_segments = segments.reshape(MICRO * ROWS, SEQ)
    flat_cot = cotangent.reshape(MICRO * ROWS, SEQ, D)
    zero_lower = tuple((jnp.zeros(w.shape, jnp.float32) for w in lower_params))
    zero_upper = tuple((jnp.zeros(w.shape, jnp.float32) for w in upper_params))

    def one_sequence(carry, item):
        total_lower, total_upper = carry
        seq_tokens, segment, seq_cot = item
        entering = seq_tokens.astype(jnp.float32)
        out_lower, back_lower = jax.vjp(lambda p, v: layer(p, v, segment), lower_params, entering)
        between = low(out_lower)
        out_upper, back_upper = jax.vjp(lambda p, v: layer(p, v, segment), upper_params, between)
        grads_upper, grad_between = back_upper(seq_cot.astype(jnp.float32))
        grads_lower, grad_entering = back_lower(grad_between)
        total_lower = tuple((a + b for a, b in zip(total_lower, grads_lower)))
        total_upper = tuple((a + b for a, b in zip(total_upper, grads_upper)))
        return ((total_lower, total_upper), (out_lower.astype(jnp.bfloat16), out_upper.astype(jnp.bfloat16), grad_entering.astype(jnp.bfloat16), grad_between.astype(jnp.bfloat16)))
    (total_lower, total_upper), (outs_lower, outs_upper, grads_in_lower, grads_in_upper) = lax.scan(one_sequence, (zero_lower, zero_upper), (flat_tokens, flat_segments, flat_cot))
    layer_out = jnp.stack([outs_lower, outs_upper]).reshape(2, MICRO, ROWS, SEQ, D)
    layer_in_grad = jnp.stack([grads_in_lower, grads_in_upper]).reshape(2, MICRO, ROWS, SEQ, D)
    stacked = [jnp.stack([a, b]) for a, b in zip(total_lower, total_upper)]
    return (layer_out, layer_in_grad, stacked[0], stacked[1], stacked[2], stacked[3], stacked[4], stacked[5], stacked[6], stacked[7], stacked[8], stacked[9], stacked[10], stacked[11])
```

```python
import functools

import jax
import jax.numpy as jnp
import ml_dtypes
import numpy as np
from jax import lax
from jax.experimental import pallas as pl
from jax.experimental.pallas import tpu as pltpu
from jax.sharding import PartitionSpec as P

HEAD_DIM = 64
LANES = 128
HALO = 64
BLOCK = 128
WINDOW = BLOCK + 2 * HALO
CHUNK = 256
TILE = 512
NEG_LARGE = -1e30
NORM_EPS = 1e-12
MESH = pl.DeviceIdType.MESH
BF = jnp.bfloat16
F32 = jnp.float32


def rotary_rows():
    place = np.arange(HALO, dtype=np.float64)[:, None]
    lane = np.arange(LANES)
    angle = place * 10000.0 ** (-2.0 * (lane % 32) / HEAD_DIM)
    sign = np.where(lane < HALO, -1.0, 1.0)
    exact = np.concatenate([np.cos(angle), np.sin(angle) * sign], axis=1).astype(np.float32)
    high = exact.astype(ml_dtypes.bfloat16)
    low = (exact - high.astype(np.float32)).astype(ml_dtypes.bfloat16)
    return np.concatenate([high, low], axis=0)


def dot(a, b):
    return lax.dot_general(a, b, (((1,), (0,)), ((), ())), preferred_element_type=F32)


def dot_t(a, b):
    return lax.dot_general(a, b, (((1,), (1,)), ((), ())), preferred_element_type=F32)


def t_dot(a, b):
    return lax.dot_general(a, b, (((0,), (0,)), ((), ())), preferred_element_type=F32)


def fold(v):
    return jnp.sum(v.reshape(v.shape[0] // 8, 8, v.shape[1]), axis=0)


def mean(v):
    return jnp.sum(v, axis=-1, keepdims=True) * (1.0 / v.shape[-1])


def standard(v):
    centred = v - mean(v)
    rstd = lax.rsqrt(mean(centred * centred) + NORM_EPS)
    return centred * rstd, rstd


def norm_back(weighted, hat, rstd):
    return rstd * (weighted - mean(weighted) - hat * mean(weighted * hat))


def pair_order(shape):
    row = lax.broadcasted_iota(jnp.int32, shape, 0)
    lane = lax.broadcasted_iota(jnp.int32, shape, 1)
    rest = lane % 64
    return (row == (rest // 32) * 64 + (rest % 32) * 2 + lane // 64).astype(F32).astype(BF)


def kernel(
    tokens, segs, cot, w_qkv, b_qkv, w_out, b_out, gain1, bias1, w_up, b_up, w_down, b_down, gain2, bias2, table,
    layer_out, in_grad, g_qkv, g_out, g_up, g_down, g_small,
    X, E, QKV, PT, CTX, HID, ACT, SL, HAT1, HAT2, R1, R2, COS, SIN, SEG, BK1, DC, CARRY,
    WQKV, WOUT, WUP, WDOWN, BQKV, LO, IG, TB, GT, SUMS,
    load_sem, x_sem, out_sem, send_f, recv_f, send_b, recv_b, grad_sem,
):
    micros, _, length, width = tokens.shape
    ff = w_up.shape[2]
    chunks = length // CHUNK
    per_chunk = CHUNK // BLOCK
    pairs = width // LANES
    sec = lax.axis_index("section")
    first = sec == 0
    other = {"section": 1 - sec}

    loads = [
        pltpu.make_async_copy(src.at[0], dst, load_sem.at[i])
        for i, (src, dst) in enumerate([(w_qkv, WQKV), (w_out, WOUT), (w_up, WUP), (w_down, WDOWN)])
    ]
    for copy in loads:
        copy.start()

    def own_rows(m):
        return (
            pltpu.make_async_copy(tokens.at[m, 0], X.at[m], x_sem.at[m]),
            pltpu.make_async_copy(cot.at[m, 0], E.at[m], x_sem.at[m]),
        )

    for m in range(micros):

        @pl.when(first)
        def _(m=m):
            own_rows(m)[0].start()

        @pl.when(jnp.logical_not(first))
        def _(m=m):
            own_rows(m)[1].start()

    barrier = pltpu.get_barrier_semaphore()
    pl.semaphore_signal(barrier, inc=1, device_id=other, device_id_type=MESH)
    pl.semaphore_wait(barrier, 1)

    def rows(c):
        return pl.ds(pl.multiple_of(c * CHUNK, CHUNK), CHUNK)

    def padded(c):
        return pl.ds(pl.multiple_of(c * CHUNK + HALO, HALO), CHUNK)

    def send_forward(m, c):
        return pltpu.make_async_remote_copy(
            src_ref=LO.at[m, rows(c), :], dst_ref=X.at[m, rows(c), :],
            send_sem=send_f.at[m, c], recv_sem=recv_f.at[m, c],
            device_id=other, device_id_type=MESH,
        )

    def send_backward(m, c):
        return pltpu.make_async_remote_copy(
            src_ref=IG.at[m, rows(c), :], dst_ref=E.at[m, rows(c), :],
            send_sem=send_b.at[m, c], recv_sem=recv_b.at[m, c],
            device_id=other, device_id_type=MESH,
        )

    def keep_out(m, c):
        return pltpu.make_async_copy(LO.at[m, rows(c), :], layer_out.at[0, m, 0, rows(c), :], out_sem.at[0, m, c])

    def keep_in(m, c):
        return pltpu.make_async_copy(IG.at[m, rows(c), :], in_grad.at[0, m, 0, rows(c), :], out_sem.at[1, m, c])

    lane_row = lax.broadcasted_iota(jnp.int32, (BLOCK, LANES), 1)
    token_row = lax.broadcasted_iota(jnp.int32, (BLOCK, LANES), 0)
    for m in range(micros):
        edge = jnp.full((HALO, LANES), -1.0, F32)
        SEG[m, :HALO, :] = edge
        SEG[m, length + HALO :, :] = edge
        for ref in (COS, SIN):
            ref[m, :HALO, :] = jnp.zeros((HALO, LANES), F32)
            ref[m, length + HALO :, :] = jnp.zeros((HALO, LANES), F32)
        blank = jnp.zeros((HALO, 3 * width), BF)
        QKV[m, :HALO, :] = blank
        QKV[m, length + HALO :, :] = blank
        for b in range(length // BLOCK):
            own = segs[m, :, b * BLOCK : (b + 1) * BLOCK].astype(F32)
            column = jnp.broadcast_to(own, (BLOCK, LANES)).T
            SEG[m, HALO + b * BLOCK : HALO + (b + 1) * BLOCK, :] = column
            ahead = (column == own) & (lane_row < token_row)
            count = ahead.astype(F32)
            if b:
                before = segs[m, :, (b - 1) * BLOCK : b * BLOCK].astype(F32)
                count += (column == before).astype(F32)
            place = jnp.sum(count, axis=-1, keepdims=True)
            pick = (place == (lane_row % HALO).astype(F32)).astype(F32).astype(BF)
            values = dot(pick, table[...])
            COS[m, HALO + b * BLOCK : HALO + (b + 1) * BLOCK, :] = values[:, :LANES]
            SIN[m, HALO + b * BLOCK : HALO + (b + 1) * BLOCK, :] = values[:, LANES:]
    SUMS[...] = jnp.zeros_like(SUMS)

    order = pair_order((LANES, LANES))
    loads[0].wait()
    BQKV[...] = jnp.broadcast_to(b_qkv[...].astype(F32), BQKV.shape)
    for j in range(2 * pairs):
        cols = slice(j * LANES, (j + 1) * LANES)
        WQKV[:, cols] = dot(WQKV[:, cols], order).astype(BF)
        BQKV[:, cols] = dot(BQKV[:, cols].astype(BF), order)
    for copy in loads[1:]:
        copy.wait()

    lane = lax.broadcasted_iota(jnp.int32, (BLOCK, LANES), 1)
    first_turned = lane % 64 < 32
    first_plain = lane < 64
    zero = jnp.zeros((BLOCK, LANES), BF)

    def two_heads(v, is_first):
        return jnp.concatenate([jnp.where(is_first, v, zero), jnp.where(is_first, zero, v)], axis=0)

    def f_qkv(m, c):
        x = X[m, rows(c), :]
        cosine, sine = COS[m, padded(c), :], SIN[m, padded(c), :]
        for g in range(3):
            cols = slice(g * width, (g + 1) * width)
            y = dot(x, WQKV[:, cols]) + BQKV[:1, cols]
            for j in range(pairs):
                v = y[:, j * LANES : (j + 1) * LANES]
                if g < 2:
                    v = v * cosine + pltpu.roll(v, 64, 1) * sine
                if g == 0:
                    v = v * HEAD_DIM**-0.5
                QKV[m, padded(c), g * width + j * LANES : g * width + (j + 1) * LANES] = v.astype(BF)

    def window(b):
        return pl.ds(pl.multiple_of(b * BLOCK, BLOCK), WINDOW)

    def queries(b):
        return pl.ds(pl.multiple_of(b * BLOCK + HALO, HALO), BLOCK)

    def f_attn(m, b):
        own = segs[m, :, pl.ds(pl.multiple_of(b * BLOCK, BLOCK), BLOCK)].astype(F32)
        shut = jnp.where(SEG[m, window(b), :] == own, 0.0, NEG_LARGE)
        shut = jnp.concatenate([shut, shut], axis=1)
        for j in range(pairs):
            q = QKV[m, queries(b), j * LANES : (j + 1) * LANES]
            k = QKV[m, window(b), width + j * LANES : width + (j + 1) * LANES]
            v = QKV[m, window(b), 2 * width + j * LANES : 2 * width + (j + 1) * LANES]
            score = dot_t(k, two_heads(q, first_turned)) + shut
            raised = jnp.exp(score - jnp.max(score, axis=0, keepdims=True))
            probs = (raised * (1.0 / jnp.sum(raised, axis=0, keepdims=True))).astype(BF)
            PT[m, b, j] = probs
            mixed = t_dot(v, probs)
            turned = jnp.concatenate([mixed[:64, :BLOCK], mixed[64:, BLOCK:]], axis=0)
            CTX[m, pl.ds(pl.multiple_of(b * BLOCK, BLOCK), BLOCK), j * LANES : (j + 1) * LANES] = turned.T.astype(BF)

    def f_rest(m, c):
        r = rows(c)
        h = X[m, r, :].astype(F32) + dot(CTX[m, r, :], WOUT[...]) + b_out[...].astype(F32)
        hat, rstd = standard(h)
        HAT1[m, r, :] = hat.astype(BF)
        R1[m, r, :] = jnp.broadcast_to(rstd, (CHUNK, LANES))
        hidden = hat * gain1[...].astype(F32) + bias1[...].astype(F32)
        low = hidden.astype(BF)
        HID[m, r, :] = low
        for n in range(0, ff, TILE):
            cols = slice(n, n + TILE)
            u = dot(low, WUP[:, cols]) + b_up[:, cols].astype(F32)
            cdf = 0.5 * lax.erf(u * 0.7071067811865476) + 0.5
            ACT[m, r, cols] = (u * cdf).astype(BF)
            SL[m, r, cols] = (cdf + u * (jnp.exp(u * u * -0.5) * 0.3989422804014327)).astype(BF)
        hat, rstd = standard(hidden + dot(ACT[m, r, :], WDOWN[...]) + b_down[...].astype(F32))
        HAT2[m, r, :] = hat.astype(BF)
        R2[m, r, :] = jnp.broadcast_to(rstd, (CHUNK, LANES))
        LO[m, r, :] = (hat * gain2[...].astype(F32) + bias2[...].astype(F32)).astype(BF)

    wide = 3 * width
    at = {}
    spot = 0
    for name, size in [("qkv", wide), ("out", width), ("gain1", width), ("bias1", width), ("up", ff), ("down", width), ("gain2", width), ("bias2", width)]:
        at[name] = slice(spot, spot + size)
        spot += size

    def add(name, v, cols=None):
        place = at[name]
        if cols is not None:
            place = slice(place.start + cols.start, place.start + cols.stop)
        SUMS[:, place] += fold(v)

    def spread(v):
        return jnp.concatenate([v] * pairs, axis=1)

    def b_ffn(m, c):
        r = rows(c)
        e = E[m, r, :].astype(F32)
        hat = HAT2[m, r, :].astype(F32)
        add("gain2", e * hat)
        add("bias2", e)
        back2 = norm_back(e * gain2[...].astype(F32), hat, spread(R2[m, r, :]))
        down = back2.astype(BF)
        E[m, r, :] = down
        add("down", down.astype(F32))
        for n in range(0, ff, TILE):
            cols = slice(n, n + TILE)
            up = (dot_t(down, WDOWN[cols, :]) * SL[m, r, cols].astype(F32)).astype(BF)
            SL[m, r, cols] = up
            add("up", up.astype(F32), cols)
        d_hidden = back2 + dot_t(SL[m, r, :], WUP[...])
        hat = HAT1[m, r, :].astype(F32)
        add("gain1", d_hidden * hat)
        add("bias1", d_hidden)
        back1 = norm_back(d_hidden * gain1[...].astype(F32), hat, spread(R1[m, r, :]))
        BK1[r, :] = back1
        mixed = back1.astype(BF)
        HAT1[m, r, :] = mixed
        add("out", mixed.astype(F32))
        DC[...] = dot_t(mixed, WOUT[...]).astype(BF)

    def turn_back(v, cosine, sine):
        return v * cosine - pltpu.roll(v, 64, 1) * sine

    def b_attn(m, b, i):
        cosine, sine = COS[m, queries(b), :], SIN[m, queries(b), :]
        done = pl.ds(pl.multiple_of(b * BLOCK, BLOCK), BLOCK)
        cosine_k, sine_k = COS[m, done, :], SIN[m, done, :]
        for j in range(pairs):
            cols = slice(j * LANES, (j + 1) * LANES)
            q = two_heads(QKV[m, queries(b), cols], first_turned)
            k = QKV[m, window(b), width + j * LANES : width + (j + 1) * LANES]
            v = QKV[m, window(b), 2 * width + j * LANES : 2 * width + (j + 1) * LANES]
            dc = two_heads(DC[i * BLOCK : (i + 1) * BLOCK, cols], first_plain)
            probs = PT[m, b, j]
            part = probs.astype(F32)
            weighted = part * dot_t(v, dc)
            score = (weighted - part * jnp.sum(weighted, axis=0, keepdims=True)).astype(BF)
            dq = t_dot(k, score)
            dq = jnp.concatenate(
                [dq[:32, :BLOCK], dq[32:64, BLOCK:], dq[64:96, :BLOCK], dq[96:, BLOCK:]], axis=0
            ).T * HEAD_DIM**-0.5
            dk = dot(score, q)
            dv = dot(probs, dc)
            QKV[m, queries(b), cols] = turn_back(dq, cosine, sine).astype(BF)
            kept_k, kept_v = CARRY[:, cols], CARRY[:, width + j * LANES : width + (j + 1) * LANES]
            QKV[m, done, width + j * LANES : width + (j + 1) * LANES] = turn_back(
                dk[:BLOCK] + kept_k, cosine_k, sine_k
            ).astype(BF)
            QKV[m, done, 2 * width + j * LANES : 2 * width + (j + 1) * LANES] = (dv[:BLOCK] + kept_v).astype(BF)
            CARRY[:, cols] = dk[BLOCK:]
            CARRY[:, width + j * LANES : width + (j + 1) * LANES] = dv[BLOCK:]

    def b_flush(m):
        last = slice(length, length + HALO)
        for j in range(pairs):
            cols = slice(j * LANES, (j + 1) * LANES)
            QKV[m, last, width + j * LANES : width + (j + 1) * LANES] = turn_back(
                CARRY[:HALO, cols], COS[m, last, :], SIN[m, last, :]
            ).astype(BF)
            QKV[m, last, 2 * width + j * LANES : 2 * width + (j + 1) * LANES] = CARRY[
                :HALO, width + j * LANES : width + (j + 1) * LANES
            ].astype(BF)

    def b_in(m, c):
        d_proj = QKV[m, padded(c), :]
        add("qkv", d_proj.astype(F32))
        IG[m, rows(c), :] = (BK1[rows(c), :] + dot_t(d_proj, WQKV[...])).astype(BF)

    def forward(m):
        @pl.when(first)
        def _():
            own_rows(m)[0].wait()

        def arrive(c):
            @pl.when(jnp.logical_not(first))
            def _():
                send_forward(m, c).wait_recv()

        arrive(0)
        f_qkv(m, 0)

        def step(c, carry):
            @pl.when(c + 1 < chunks)
            def _():
                arrive(c + 1)
                f_qkv(m, c + 1)

            for i in range(per_chunk):
                f_attn(m, c * per_chunk + i)
            f_rest(m, c)
            keep_out(m, c).start()

            @pl.when(first)
            def _():
                send_forward(m, c).start()

            return carry

        lax.fori_loop(0, chunks, step, 0)

    def backward(m):
        @pl.when(jnp.logical_not(first))
        def _():
            own_rows(m)[1].wait()

        CARRY[...] = jnp.zeros_like(CARRY)

        def leave(c):
            b_in(m, c)
            keep_in(m, c).start()

            @pl.when(jnp.logical_not(first))
            def _():
                send_backward(m, c).start()

        def step(c, carry):
            @pl.when(first)
            def _():
                send_backward(m, c).wait_recv()

            b_ffn(m, c)
            for i in range(per_chunk):
                b_attn(m, c * per_chunk + i, i)

            @pl.when(c > 0)
            def _():
                leave(c - 1)

            return carry

        lax.fori_loop(0, chunks, step, 0)
        b_flush(m)
        leave(chunks - 1)

    def phase(step, carry):
        m = jnp.where(first, step % 2, step // 2)
        turn = jnp.where(first, step // 2, step % 2)

        @pl.when(turn == 0)
        def _():
            forward(m)

        @pl.when(turn == 1)
        def _():
            backward(m)

        return carry

    lax.fori_loop(0, 2 * micros, phase, 0)

    def turned(ref):
        for m in range(micros):
            TB[:, m * length : (m + 1) * length] = ref[m].T

    def total(ref, cols, shift=0):
        return sum(
            dot(TB[:, m * length : (m + 1) * length], ref[m, shift : shift + length, cols]) for m in range(micros)
        )

    turned(E)
    for n in range(0, ff, TILE):
        GT[n : n + TILE, :width] = total(ACT, slice(n, n + TILE)).T
    store_down = pltpu.make_async_copy(GT.at[:, pl.ds(0, width)], g_down.at[0], grad_sem.at[0])
    store_down.start()
    turned(HID)
    store_down.wait()
    for n in range(0, ff, TILE):
        LOW = total(SL, slice(n, n + TILE))
        GT[n : n + width, :TILE] = LOW
    stores = [
        pltpu.make_async_copy(GT.at[pl.ds(n, width), pl.ds(0, TILE)], g_up.at[0, :, pl.ds(n, TILE)], grad_sem.at[1 + i])
        for i, n in enumerate(range(0, ff, TILE))
    ]
    for s in stores:
        s.start()
    turned(CTX)
    for s in stores:
        s.wait()
    GT[:width, :width] = total(HAT1, slice(0, width))
    turned(X)
    for g in range(3):
        part = total(QKV, slice(g * width, (g + 1) * width), HALO)
        if g < 2:
            part = jnp.concatenate(
                [dot_t(part[:, j * LANES : (j + 1) * LANES].astype(BF), order) for j in range(pairs)], axis=1
            )
        GT[(g + 1) * width : (g + 2) * width, :width] = part
    stores = [pltpu.make_async_copy(GT.at[pl.ds(0, width), pl.ds(0, width)], g_out.at[0], grad_sem.at[0])]
    stores += [
        pltpu.make_async_copy(
            GT.at[pl.ds((g + 1) * width, width), pl.ds(0, width)], g_qkv.at[0, :, pl.ds(g * width, width)], grad_sem.at[1 + g]
        )
        for g in range(3)
    ]
    for s in stores:
        s.start()
    small = jnp.sum(SUMS[...], axis=0, keepdims=True)
    g_small[...] = small
    high = jnp.broadcast_to(small[:, : 2 * width], (16, 2 * width))
    for j in range(2 * pairs):
        cols = slice(j * LANES, (j + 1) * LANES)
        top = high[:, cols].astype(BF)
        rest = (high[:, cols] - top.astype(F32)).astype(BF)
        g_small[:, cols] = (dot_t(top, order) + dot_t(rest, order))[:1]
    for s in stores:
        s.wait()

    def finish(i, carry):
        m, c = i // chunks, i % chunks
        keep_out(m, c).wait()
        keep_in(m, c).wait()

        @pl.when(first)
        def _():
            send_forward(m, c).wait_send()

        @pl.when(jnp.logical_not(first))
        def _():
            send_backward(m, c).wait_send()

        return carry

    lax.fori_loop(0, micros * chunks, finish, 0)


def body(tokens, segments, cotangent, *params):
    micros, _, length, width = tokens.shape
    ff = params[6].shape[2]
    chunks, blocks, pairs = length // CHUNK, length // BLOCK, width // LANES
    small = 3 * width + 6 * width + ff
    any_space, vmem = pl.BlockSpec(memory_space=pl.ANY), pl.BlockSpec(memory_space=pltpu.VMEM)
    big = {0, 3, 5, 9, 11}
    specs = [any_space, vmem, any_space]
    specs += [any_space if i in (0, 2, 6, 8) else vmem for i in range(12)] + [vmem]
    table = jnp.asarray(rotary_rows())

    def scratch(*shape, dtype=BF):
        return pltpu.VMEM(shape, dtype)

    row = (micros, length, width)
    scratches = [
        scratch(*row), scratch(*row), scratch(micros, length + 2 * HALO, 3 * width),
        scratch(micros, blocks, pairs, WINDOW, 2 * BLOCK), scratch(*row), scratch(*row),
        scratch(micros, length, ff), scratch(micros, length, ff), scratch(*row), scratch(*row),
        scratch(micros, length, LANES, dtype=F32), scratch(micros, length, LANES, dtype=F32),
        scratch(micros, length + 2 * HALO, LANES, dtype=F32), scratch(micros, length + 2 * HALO, LANES, dtype=F32),
        scratch(micros, length + 2 * HALO, LANES, dtype=F32),
        scratch(length, width, dtype=F32), scratch(CHUNK, width), scratch(BLOCK, 2 * width, dtype=F32),
        scratch(width, 3 * width), scratch(width, width), scratch(width, ff), scratch(ff, width),
        scratch(16, 3 * width, dtype=F32), scratch(*row), scratch(*row),
        scratch(width, micros * length), scratch(ff, TILE, dtype=F32), scratch(8, small, dtype=F32),
        pltpu.SemaphoreType.DMA((4,)), pltpu.SemaphoreType.DMA((micros,)), pltpu.SemaphoreType.DMA((2, micros, chunks)),
        pltpu.SemaphoreType.DMA((micros, chunks)), pltpu.SemaphoreType.DMA((micros, chunks)),
        pltpu.SemaphoreType.DMA((micros, chunks)), pltpu.SemaphoreType.DMA((micros, chunks)),
        pltpu.SemaphoreType.DMA((4,)),
    ]
    S = jax.ShapeDtypeStruct
    outs = (
        S((1,) + tokens.shape, BF), S((1,) + tokens.shape, BF),
        S((1, width, 3 * width), F32), S((1, width, width), F32), S((1, width, ff), F32), S((1, ff, width), F32),
        S((1, small), F32),
    )
    layer_out, in_grad, g_qkv, g_out, g_up, g_down, g_small = pl.pallas_call(
        kernel,
        out_shape=outs,
        in_specs=specs,
        out_specs=(any_space,) * 6 + (vmem,),
        scratch_shapes=scratches,
        compiler_params=pltpu.CompilerParams(
            collective_id=0, has_side_effects=True, vmem_limit_bytes=64 * 1024 * 1024
        ),
        name="relay",
    )(tokens, segments, cotangent, *params, table)
    g_qkv, g_out, g_up, g_down, g_small = lax.psum((g_qkv, g_out, g_up, g_down, g_small), "batch")
    sizes = [3 * width, width, width, width, ff, width, width, width]
    ends = np.cumsum(sizes)
    s_qkv, s_out, s_gain1, s_bias1, s_up, s_down, s_gain2, s_bias2 = (
        g_small[:, e - n : e] for e, n in zip(ends, sizes)
    )
    return (
        layer_out, in_grad, g_qkv, s_qkv, g_out, s_out, s_gain1, s_bias1,
        g_up, s_up, g_down, s_down, s_gain2, s_bias2,
    )


def solution(mesh):
    rows, ids = P(None, "batch", None, None), P(None, "batch", None)
    matrix, vector = P("section", None, None), P("section", None)
    weights = (matrix, vector, matrix, vector, vector, vector, matrix, vector, matrix, vector, vector, vector)
    kept = P("section", None, "batch", None, None)
    return jax.shard_map(
        body,
        mesh=mesh,
        in_specs=(rows, ids, rows) + weights,
        out_specs=(kept, kept) + weights,
        check_vma=False,
    )
```
